512 devices in a mesh: dp: 32 (over y_lo, x, core), mp: 16 (over z, y_hi).
Axes of the slice: x: 4, y: 8 (y_hi: 2, y_lo: 4; y = y_hi * 4 + y_lo), z: 8, core: 2. Of those that a mesh axis runs over, the one named last changes fastest.
Arguments:
- query_rows: bfloat16 [8192, 4096], P('dp', 'mp'), may hold values from -8.5 to 8.5
- key_rows: bfloat16 [8192, 4096], P('dp', 'mp'), may hold values from -8.5 to 8.5
- value_rows: bfloat16 [8192, 4096], P('dp', 'mp'), may hold values from -12 to 12
- out_weight: bfloat16 [4096, 6144], P('mp', 'dp'), may hold values from -0.1875 to 0.1875
- grad_out: bfloat16 [8192, 6144], P('dp', 'mp'), may hold values from -6 to 6
Outputs:
- layer_out: bfloat16 [8192, 6144], P('dp', 'mp')
- grad_query: bfloat16 [8192, 4096], P('dp', 'mp')
- grad_key: bfloat16 [8192, 4096], P('dp', 'mp')
- grad_value: bfloat16 [8192, 4096], P('dp', 'mp')
- grad_weight: float32 [4096, 6144], P('mp', 'dp')
The draws below stay inside these ranges and needn't reach their ends.
All inputs are finite; a program needn't handle non-finite values.
Results may differ from the reference program's by a relative error of at most 0.019.
Values may be sent and summed in bfloat16 or wider, within the bound.
No kernel may reach another device: no remote copies, remote signals or barrier semaphores. Data moves between devices by JAX's collectives and lax.ppermute only.
A program may use at most 64 MiB of HBM per device.

```python
import math
import jax
import jax.numpy as jnp
from jax import lax

D = 6144
HEADS = 32
HEAD = 128
PATCHES = 256
HD = 4096
TOK_DEV = 256
TOKENS = 8192
N_DP = 32
N_MP = 16


def draw_query_rows(key, part):
    key = jax.random.fold_in(key, 7)
    values = jnp.clip(jax.random.normal(key, (TOKENS, HD), jnp.float32), -4.0, 4.0)
    return values.astype(jnp.bfloat16)


def draw_key_rows(key, part):
    key = jax.random.fold_in(key, 9)
    values = jnp.clip(jax.random.normal(key, (TOKENS, HD), jnp.float32), -4.0, 4.0)
    return values.astype(jnp.bfloat16)


def with_spikes(array, key, source, target, blocks, factor):
    def block_of(dim):
        return (jnp.arange(array.shape[dim]) // (array.shape[dim] // blocks)).reshape((-1,) + (1,) * (array.ndim - 1 - dim))

    first = jax.random.permutation(key, blocks)[block_of(target)]
    far = (block_of(target) + blocks // 2) % blocks
    return jnp.where((block_of(source) == first) | (block_of(source) == far), factor * array, array)


def level_of(stream_key, dims, cuts, low, top_value):
    level, own = 1.0, jax.random.fold_in(stream_key, 6)
    for axis_at, parts in cuts:
        draws = jnp.exp(jax.random.uniform(jax.random.fold_in(own, axis_at), (parts,), jnp.float32, low / len(cuts), top_value / len(cuts)))
        level = level * jnp.repeat(draws, dims[axis_at] // parts).reshape([-1 if axis == axis_at else 1 for axis in range(len(dims))])
    return level


def scatter_about(stream_key, extent, deviation, bound, cuts=(), kind=jnp.bfloat16):
    loudness = level_of(stream_key, extent, cuts, -0.22, 0.18) if cuts else 1.0
    array = jax.random.normal(stream_key, extent, jnp.float32) * deviation * loudness
    return jnp.minimum(jnp.maximum(array, -bound), bound).astype(kind)


def bell_draw_with(stream_key, shape, spread, reach, shards, heavy, held_as=jnp.bfloat16):
    values = spread * jax.random.normal(stream_key, shape, jnp.float32)
    if shards:
        values = values * level_of(stream_key, shape, shards, -0.22, 0.18)
    return jnp.clip(with_spikes(values, jax.random.fold_in(stream_key, 3), *heavy), -reach, reach).astype(held_as)


def setup_inputs(seed: int = 0) -> dict:
    seeds = jax.random.split(jax.random.key(seed), 6)
    return {
        "query_rows": draw_query_rows(jax.random.fold_in(seeds[5], 71), 0),
        "key_rows": draw_key_rows(jax.random.fold_in(seeds[5], 71), 0),
        "value_rows": scatter_about(seeds[2], (TOKENS, HD), 2.0, 12.0, ((0, 32), (1, 16))),
        "out_weight": bell_draw_with(seeds[3], (HD, D), HD ** -0.5, 0.1875, ((0, 16), (1, 32)), (0, 1, 32, 2.75)),
        "grad_out": bell_draw_with(seeds[4], (TOKENS, D), 0.25, 6.0, ((0, 32), (1, 16)), (0, 1, 32, 2.75)),
    }


def to_low(values):
    return lax.optimization_barrier(values.astype(jnp.bfloat16))

def reference(query_rows, key_rows, value_rows, out_weight, grad_out):
    factor = 1.0 / math.sqrt(HEAD)
    images = TOKENS // PATCHES
    shaped = (images, PATCHES, HEADS, HEAD)
    dcontext = jnp.dot(grad_out, out_weight.T, preferred_element_type=jnp.float32).astype(jnp.bfloat16)

    def per_image(inputs):
        query_img, key_img, value_img, dctx_img = inputs
        query_wide = query_img.astype(jnp.float32)
        key_wide = key_img.astype(jnp.float32)
        value_wide = value_img.astype(jnp.float32)
        dctx_wide = dctx_img.astype(jnp.float32)
        scores = jnp.einsum('qhd,khd->hqk', query_wide, key_wide) * factor
        maximum = lax.optimization_barrier(jnp.max(scores, axis=-1, keepdims=True))
        exponent = jnp.exp(scores - maximum)
        probs = exponent / lax.optimization_barrier(jnp.sum(exponent, axis=-1, keepdims=True))
        probs_low = to_low(probs).astype(jnp.float32)
        context = jnp.einsum('hqk,khd->qhd', probs_low, value_wide).astype(jnp.bfloat16)
        grad_value = jnp.einsum('hqk,qhd->khd', probs_low, dctx_wide).astype(jnp.bfloat16)
        dprobs = jnp.einsum('qhd,khd->hqk', dctx_wide, value_wide)
        center = lax.optimization_barrier(jnp.sum(probs * dprobs, axis=-1, keepdims=True))
        dscores = to_low(probs * (dprobs - center)).astype(jnp.float32)
        grad_query = (jnp.einsum('hqk,khd->qhd', dscores, key_wide) * factor).astype(jnp.bfloat16)
        grad_key = (jnp.einsum('hqk,qhd->khd', dscores, query_wide) * factor).astype(jnp.bfloat16)
        return (context, grad_query, grad_key, grad_value)
    results = lax.map(per_image, (query_rows.reshape(shaped), key_rows.reshape(shaped), value_rows.reshape(shaped), dcontext.reshape(shaped)))
    context, grad_query, grad_key, grad_value = [item.reshape(TOKENS, HD) for item in results]
    width = HD // N_MP

    def head_group(running, group):
        columns = lax.dynamic_slice_in_dim(context, group * width, width, 1)
        rows = lax.dynamic_slice_in_dim(out_weight, group * width, width, 0)
        partial_sum = to_low(jnp.dot(columns, rows, preferred_element_type=jnp.float32))
        return (running + partial_sum.astype(jnp.float32), None)
    summed, unused = lax.scan(head_group, jnp.zeros((TOKENS, D), jnp.float32), jnp.arange(N_MP, dtype=jnp.int32))
    layer_out = summed.astype(jnp.bfloat16)

    def token_group(running, group):
        ctx_rows = lax.dynamic_slice_in_dim(context, group * TOK_DEV, TOK_DEV, 0)
        cot_rows = lax.dynamic_slice_in_dim(grad_out, group * TOK_DEV, TOK_DEV, 0)
        term = lax.dot_general(ctx_rows, cot_rows, (((0,), (0,)), ((), ())), preferred_element_type=jnp.float32)
        return (running + to_low(term).astype(jnp.float32), None)
    grad_weight, unused_two = lax.scan(token_group, jnp.zeros((HD, D), jnp.float32), jnp.arange(N_DP, dtype=jnp.int32))
    return (layer_out, grad_query, grad_key, grad_value, grad_weight)
```

```python
import math

import jax
import jax.numpy as jnp
from jax import lax
from jax.sharding import Mesh, PartitionSpec as P

HEAD = 128
PATCHES = 256
AXES = ("y_lo", "x", "core", "z_hi", "z_lo", "y_hi")
SIZES = (4, 4, 2, 4, 2, 2)
ROWS = ("y_lo", "x", "core")
COLS = ("z_hi", "z_lo", "y_hi")
BF16 = jnp.bfloat16
F32 = jnp.float32


def swap_pairs():
    return [(p * 4 + q, q * 4 + p) for p in range(4) for q in range(4)]


def gather(block, axis, count):
    wide = jnp.broadcast_to(block[None], (count,) + block.shape)
    return lax.all_to_all(wide, axis, split_axis=0, concat_axis=0, tiled=True)


def scatter(blocks, axis):
    return lax.all_to_all(blocks, axis, split_axis=0, concat_axis=0, tiled=True)


def total(blocks):
    return blocks.astype(F32).sum(axis=0)


def other_core(block):
    return lax.ppermute(block, "core", [(0, 1), (1, 0)])


def local(query_rows, key_rows, value_rows, out_weight, grad_out):
    factor = 1.0 / math.sqrt(HEAD)
    core = lax.axis_index("core")

    weight = lax.ppermute(out_weight.T, ("y_lo", "z_hi"), swap_pairs())
    weight = gather(weight, "y_lo", 4)
    weight = gather(weight, "x", 4)
    far = other_core(weight)
    first = jnp.where(core == 0, weight, far)
    second = jnp.where(core == 0, far, weight)
    weight = jnp.stack([first, second], axis=2)
    weight = weight.reshape(4, 4, 384, 256)

    cot = gather(grad_out, ("z_lo", "y_hi"), 4)

    heads = lambda v: v.reshape(PATCHES, 2, HEAD)
    query, key, value = heads(query_rows), heads(key_rows), heads(value_rows)
    scores = jnp.einsum("qhd,khd->hqk", query, key, preferred_element_type=F32) * factor
    maximum = jnp.max(scores, axis=-1, keepdims=True)
    exponent = jnp.exp(scores - maximum)
    probs = exponent / jnp.sum(exponent, axis=-1, keepdims=True)
    probs_low = probs.astype(BF16)
    context = jnp.einsum("hqk,khd->qhd", probs_low, value, preferred_element_type=F32)
    context = context.astype(BF16).reshape(PATCHES, 2 * HEAD)
    ctx = gather(context, "z_hi", 4)

    term = jnp.einsum("xrn,ark->xank", cot, ctx, preferred_element_type=F32).astype(BF16)
    term = term.reshape(4, 4, 2, 192, 256)
    mine = jnp.where(core == 0, term[:, :, 0], term[:, :, 1])
    theirs = jnp.where(core == 0, term[:, :, 1], term[:, :, 0])
    term = (mine.astype(F32) + other_core(theirs).astype(F32)).astype(BF16)
    term = total(scatter(term, "x")).astype(BF16)
    term = total(scatter(term, "y_lo")).astype(BF16)
    term = lax.ppermute(term, ("y_lo", "z_hi"), swap_pairs())
    grad_weight = term.T.astype(F32)

    dctx = jnp.einsum("xrn,xank->ark", cot, weight, preferred_element_type=F32).astype(BF16)
    dctx = total(scatter(dctx, "z_hi")).astype(BF16)
    out = jnp.einsum("ark,xank->xrn", ctx, weight, preferred_element_type=F32).astype(BF16)
    layer_out = total(scatter(out, ("z_lo", "y_hi"))).astype(BF16)

    dctx = heads(dctx)
    grad_value = jnp.einsum("hqk,qhd->khd", probs_low, dctx, preferred_element_type=F32)
    dprobs = jnp.einsum("qhd,khd->hqk", dctx, value, preferred_element_type=F32)
    center = jnp.sum(probs * dprobs, axis=-1, keepdims=True)
    dscores = (probs * (dprobs - center)).astype(BF16)
    grad_query = jnp.einsum("hqk,khd->qhd", dscores, key, preferred_element_type=F32) * factor
    grad_key = jnp.einsum("hqk,qhd->khd", dscores, query, preferred_element_type=F32) * factor
    flat = lambda v: v.astype(BF16).reshape(PATCHES, 2 * HEAD)
    return (layer_out, flat(grad_query), flat(grad_key), flat(grad_value), grad_weight)


def solution(mesh):
    fine = Mesh(mesh.devices.reshape(SIZES), AXES)
    rows_cols, cols_rows = P(ROWS, COLS), P(COLS, ROWS)
    in_specs = (rows_cols, rows_cols, rows_cols, cols_rows, rows_cols)
    out_specs = (rows_cols, rows_cols, rows_cols, rows_cols, cols_rows)
    return jax.shard_map(local, mesh=fine, in_specs=in_specs, out_specs=out_specs, check_vma=False)
```

```python
import math

import jax
import jax.numpy as jnp
from jax import lax
from jax.experimental import pallas as pl
from jax.experimental.pallas import tpu as pltpu
from jax.sharding import Mesh, PartitionSpec as P

HEAD = 128
PATCHES = 256
FACTOR = 1.0 / math.sqrt(HEAD)
AXES = ("y_lo", "x", "core", "z", "y_hi")
SIZES = (4, 4, 2, 8, 2)
ROWS = ("y_lo", "x", "core")
COLS = ("z", "y_hi")
BF16 = jnp.bfloat16
F32 = jnp.float32
STRIP = 192
TN = (((0,), (0,)), ((), ()))
NT = (((1,), (1,)), ((), ()))
NN = (((1,), (0,)), ((), ()))


def dot(a, b, dims):
    return lax.dot_general(a, b, dims, preferred_element_type=F32)


def call(body, outs, scratch, flops, size, n_in, scalars=False, vmem_mib=40):
    vmem = pl.BlockSpec(memory_space=pltpu.VMEM)
    smem = pl.BlockSpec(memory_space=pltpu.SMEM)
    return pl.pallas_call(
        body,
        out_shape=[jax.ShapeDtypeStruct(s, t) for s, t in outs],
        in_specs=([smem] if scalars else []) + [vmem] * n_in,
        out_specs=[vmem] * len(outs),
        scratch_shapes=scratch,
        compiler_params=pltpu.CompilerParams(vmem_limit_bytes=vmem_mib * 2**20),
        cost_estimate=pl.CostEstimate(flops=flops, bytes_accessed=size, transcendentals=0),
    )


def attend(q_ref, k_ref, v_ref, ctx_ref, probs_ref):
    for h in range(2):
        cols = slice(h * HEAD, (h + 1) * HEAD)
        scores = dot(q_ref[:, cols], k_ref[:, cols], NT) * FACTOR
        exponent = jnp.exp(scores - jnp.max(scores, axis=-1, keepdims=True))
        probs = exponent / jnp.sum(exponent, axis=-1, keepdims=True)
        probs_ref[h] = probs
        ctx_ref[:, cols] = dot(probs.astype(BF16), v_ref[:, cols], NN).astype(BF16)


def attend_back(q_ref, k_ref, v_ref, probs_ref, dctx_ref, gq_ref, gk_ref, gv_ref):
    for h in range(2):
        cols = slice(h * HEAD, (h + 1) * HEAD)
        dctx = dctx_ref[:, cols]
        probs = probs_ref[h]
        gv_ref[:, cols] = dot(probs.astype(BF16), dctx, TN).astype(BF16)
        dprobs = dot(dctx, v_ref[:, cols], NT)
        center = jnp.sum(probs * dprobs, axis=-1, keepdims=True)
        dscores = (probs * (dprobs - center)).astype(BF16)
        gq_ref[:, cols] = (dot(dscores, k_ref[:, cols], NN) * FACTOR).astype(BF16)
        gk_ref[:, cols] = (dot(dscores, q_ref[:, cols], TN) * FACTOR).astype(BF16)


def turn_cot(where_ref, own_ref, far_ref, mine_ref, theirs_ref, work):
    core = where_ref[0]
    for slot, cot in enumerate((own_ref, far_ref)):
        work[...] = cot[...].astype(F32).T.astype(BF16)
        rows = slice(slot * STRIP, (slot + 1) * STRIP)
        mine_ref[rows, :] = work[pl.ds(pl.multiple_of(core * STRIP, 16), STRIP), :]
        theirs_ref[rows, :] = work[pl.ds(pl.multiple_of((1 - core) * STRIP, 16), STRIP), :]


def weight_term(where_ref, ctx_ref, other_ctx_ref, cot_ref, other_cot_ref, term_ref):
    half = where_ref[1]
    for z in range(8):
        term = dot(cot_ref[...], ctx_ref[z], NN) + dot(other_cot_ref[...], other_ctx_ref[z], NN)
        for slot in range(2):
            x = 2 * (z % 2) + (half if slot == 0 else 1 - half)
            term_ref[x, z // 2] = term[slot * STRIP : (slot + 1) * STRIP].astype(BF16)


def add_up(blocks_ref, sum_ref):
    for y in range(4):
        sum_ref[y] = sum(blocks_ref[x, y].astype(F32) for x in range(4)).astype(BF16)


def project(
    where_ref, ctx_ref, own_ref, far_ref, near_w_ref, far_w_ref,
    dctx_ref, keep_ref, send_ref, weight, ctx
):
    core, half = where_ref[0], where_ref[1]
    near_row = pl.multiple_of(core * STRIP, 16)
    far_row = pl.multiple_of((1 - core) * STRIP, 16)
    for z in range(8):
        cols = slice(z * 256, (z + 1) * 256)
        ctx[:, cols] = ctx_ref[z]
        for slot in range(2):
            x = 2 * (z % 2) + (half if slot == 0 else 1 - half)
            weight[slot, pl.ds(near_row, STRIP), cols] = near_w_ref[x, z // 2]
            weight[slot, pl.ds(far_row, STRIP), cols] = far_w_ref[x, z // 2]
    for z in range(8):
        cols = slice(z * 256, (z + 1) * 256)
        part = dot(own_ref[...], weight[0, :, cols], NN) + dot(far_ref[...], weight[1, :, cols], NN)
        dctx_ref[z] = part.astype(BF16)
    keep_ref[...] = dot(ctx[...], weight[0], NT).astype(BF16)
    send_ref[...] = dot(ctx[...], weight[1], NT).astype(BF16)


def plane_pairs():
    pairs = []
    for y in range(4):
        for x in range(4):
            for z in range(8):
                there = (z // 2, 2 * (z % 2) + x % 2, 2 * y + x // 2)
                pairs.append(((y * 4 + x) * 8 + z, (there[0] * 4 + there[1]) * 8 + there[2]))
    return pairs


def change_plane(block):
    return lax.ppermute(block, ("y_lo", "x", "z"), plane_pairs())


def gather(block, axis, count):
    wide = jnp.broadcast_to(block[None], (count,) + block.shape)
    return lax.all_to_all(wide, axis, split_axis=0, concat_axis=0, tiled=True)


def scatter(blocks, axis):
    return lax.all_to_all(blocks, axis, split_axis=0, concat_axis=0, tiled=True)


def total(blocks):
    return sum(b.astype(F32) for b in blocks)


def swap(block, axis):
    return lax.ppermute(block, axis, [(0, 1), (1, 0)])


def local(query_rows, key_rows, value_rows, out_weight, grad_out):
    core, half = lax.axis_index("core"), lax.axis_index("y_hi")
    where = jnp.stack([core, half]).astype(jnp.int32)
    square = ((256, 256), BF16)
    wide = ((256, 384), BF16)

    context, probs = call(
        attend, [square, ((2, 256, 256), F32)], [], 2**26, 2**20, 3, vmem_mib=60
    )(query_rows, key_rows, value_rows)
    ctx = lax.all_gather(context, "z", axis=0)

    weight = change_plane(out_weight.T)
    grad_out, context = lax.optimization_barrier((grad_out, context))
    far_cot = swap(grad_out, "y_hi")
    weight = lax.all_gather(weight, "y_lo", axis=0)
    weight, far_cot = lax.optimization_barrier((weight, far_cot))
    near = gather(weight, "x", 4)

    strips = ((2 * STRIP, 256), BF16)
    cot_mine, cot_theirs = call(
        turn_cot, [strips, strips], [pltpu.VMEM((384, 256), BF16)], 2**20, 2**20, 2, True, vmem_mib=4
    )(where, grad_out, far_cot)
    other_cot = swap(cot_theirs, "core")
    other_ctx = swap(ctx, "core")
    term = call(
        weight_term, [((4, 4, STRIP, 256), BF16)], [], 2**29, 2**22, 4, True, vmem_mib=60
    )(where, ctx, other_ctx, cot_mine, other_cot)[0]
    near, term = lax.optimization_barrier((near, term))
    far = swap(near, "core")
    term = scatter(term, "x")
    term = call(add_up, [((4, STRIP, 256), BF16)], [], 2**20, 2**21, 1, vmem_mib=4)(term)[0]

    dctx, keep, send = call(
        project,
        [((8, 256, 256), BF16), wide, wide],
        [pltpu.VMEM((2, 384, 2048), BF16), pltpu.VMEM((256, 2048), BF16)],
        2**30,
        2**23,
        5,
        True,
        vmem_mib=60,
    )(where, ctx, grad_out, far_cot, near, far)
    dctx = lax.psum_scatter(dctx, "z", scatter_dimension=0, tiled=True)[0]
    received = swap(send, "y_hi")
    layer_out = total([keep, received]).astype(BF16)
    term, received = lax.optimization_barrier((term, received))
    term = total(scatter(term, "y_lo")).astype(BF16)
    grad_weight = change_plane(term).T.astype(F32)
    grad_query, grad_key, grad_value = call(
        attend_back, [square] * 3, [], 2**27, 2**21, 5, vmem_mib=60
    )(query_rows, key_rows, value_rows, probs, dctx)
    return (layer_out, grad_query, grad_key, grad_value, grad_weight)


def solution(mesh):
    fine = Mesh(mesh.devices.reshape(SIZES), AXES)
    rows_cols, cols_rows = P(ROWS, COLS), P(COLS, ROWS)
    in_specs = (rows_cols, rows_cols, rows_cols, cols_rows, rows_cols)
    out_specs = (rows_cols, rows_cols, rows_cols, rows_cols, cols_rows)
    return jax.shard_map(local, mesh=fine, in_specs=in_specs, out_specs=out_specs, check_vma=False)
```

```python
import math

import jax
import jax.numpy as jnp
from jax import lax
from jax.experimental import pallas as pl
from jax.experimental.pallas import tpu as pltpu
from jax.sharding import Mesh, PartitionSpec as P

HEAD = 128
PATCHES = 256
FACTOR = 1.0 / math.sqrt(HEAD)
AXES = ("y_lo", "x", "core", "z", "y_hi")
SIZES = (4, 4, 2, 8, 2)
ROWS = ("y_lo", "x", "core")
COLS = ("z", "y_hi")
BF16 = jnp.bfloat16
F32 = jnp.float32
STRIP = 192
TN = (((0,), (0,)), ((), ()))
NT = (((1,), (1,)), ((), ()))
NN = (((1,), (0,)), ((), ()))


def dot(a, b, dims):
    return lax.dot_general(a, b, dims, preferred_element_type=F32)


def call(body, outs, scratch, flops, size, n_in, scalars=False, vmem_mib=40):
    vmem = pl.BlockSpec(memory_space=pltpu.VMEM)
    smem = pl.BlockSpec(memory_space=pltpu.SMEM)
    return pl.pallas_call(
        body,
        out_shape=[jax.ShapeDtypeStruct(s, t) for s, t in outs],
        in_specs=([smem] if scalars else []) + [vmem] * n_in,
        out_specs=[vmem] * len(outs),
        scratch_shapes=scratch,
        compiler_params=pltpu.CompilerParams(vmem_limit_bytes=vmem_mib * 2**20),
        cost_estimate=pl.CostEstimate(flops=flops, bytes_accessed=size, transcendentals=0),
    )


def attend(q_ref, k_ref, v_ref, ctx_ref, probs_ref):
    for h in range(2):
        cols = slice(h * HEAD, (h + 1) * HEAD)
        scores = dot(q_ref[:, cols], k_ref[:, cols], NT) * FACTOR
        exponent = jnp.exp(scores - jnp.max(scores, axis=-1, keepdims=True))
        probs = exponent / jnp.sum(exponent, axis=-1, keepdims=True)
        probs_ref[h] = probs
        ctx_ref[:, cols] = dot(probs.astype(BF16), v_ref[:, cols], NN).astype(BF16)


def attend_back(q_ref, k_ref, v_ref, probs_ref, dctx_ref, gq_ref, gk_ref, gv_ref):
    for h in range(2):
        cols = slice(h * HEAD, (h + 1) * HEAD)
        dctx = dctx_ref[:, cols]
        probs = probs_ref[h]
        gv_ref[:, cols] = dot(probs.astype(BF16), dctx, TN).astype(BF16)
        dprobs = dot(dctx, v_ref[:, cols], NT)
        center = jnp.sum(probs * dprobs, axis=-1, keepdims=True)
        dscores = (probs * (dprobs - center)).astype(BF16)
        gq_ref[:, cols] = (dot(dscores, k_ref[:, cols], NN) * FACTOR).astype(BF16)
        gk_ref[:, cols] = (dot(dscores, q_ref[:, cols], TN) * FACTOR).astype(BF16)


def turn_cot(where_ref, own_ref, far_ref, mine_ref, theirs_ref, work):
    core = where_ref[0]
    for slot, cot in enumerate((own_ref, far_ref)):
        work[...] = cot[...].astype(F32).T.astype(BF16)
        rows = slice(slot * STRIP, (slot + 1) * STRIP)
        mine_ref[rows, :] = work[pl.ds(pl.multiple_of(core * STRIP, 16), STRIP), :]
        theirs_ref[rows, :] = work[pl.ds(pl.multiple_of((1 - core) * STRIP, 16), STRIP), :]


def weight_term(where_ref, ctx_ref, other_ctx_ref, cot_ref, other_cot_ref, term_ref):
    half = where_ref[1]
    for z in range(8):
        term = dot(cot_ref[...], ctx_ref[z], NN) + dot(other_cot_ref[...], other_ctx_ref[z], NN)
        for slot in range(2):
            x = 2 * (z % 2) + (half if slot == 0 else 1 - half)
            term_ref[x, z // 2] = term[slot * STRIP : (slot + 1) * STRIP].astype(BF16)


def add_up(blocks_ref, sum_ref):
    for y in range(4):
        sum_ref[y] = sum(blocks_ref[x, y].astype(F32) for x in range(4)).astype(BF16)


def project_back(where_ref, mine_ref, theirs_ref, near_w_ref, far_w_ref, dctx_ref):
    half = where_ref[1]
    for z in range(8):
        part = None
        for slot in range(2):
            x = 2 * (z % 2) + (half if slot == 0 else 1 - half)
            rows = slice(slot * STRIP, (slot + 1) * STRIP)
            both = dot(mine_ref[rows, :], near_w_ref[x, z // 2], TN) + dot(
                theirs_ref[rows, :], far_w_ref[x, z // 2], TN
            )
            part = both if part is None else part + both
        dctx_ref[z] = part.astype(BF16)


def project(where_ref, ctx_ref, near_w_ref, far_w_ref, keep_ref, send_ref):
    core, half = where_ref[0], where_ref[1]
    for slot, out_ref in enumerate((keep_ref, send_ref)):
        x_lo = half if slot == 0 else 1 - half
        mine, theirs = (
            sum(dot(ctx_ref[z], w_ref[2 * (z % 2) + x_lo, z // 2], NT) for z in range(8)).astype(BF16)
            for w_ref in (near_w_ref, far_w_ref)
        )
        out_ref[:, :STRIP] = jnp.where(core == 0, mine, theirs)
        out_ref[:, STRIP:] = jnp.where(core == 0, theirs, mine)


def plane_pairs():
    pairs = []
    for y in range(4):
        for x in range(4):
            for z in range(8):
                there = (z // 2, 2 * (z % 2) + x % 2, 2 * y + x // 2)
                pairs.append(((y * 4 + x) * 8 + z, (there[0] * 4 + there[1]) * 8 + there[2]))
    return pairs


def change_plane(block):
    return lax.ppermute(block, ("y_lo", "x", "z"), plane_pairs())


def gather(block, axis, count):
    wide = jnp.broadcast_to(block[None], (count,) + block.shape)
    return lax.all_to_all(wide, axis, split_axis=0, concat_axis=0, tiled=True)


def scatter(blocks, axis):
    return lax.all_to_all(blocks, axis, split_axis=0, concat_axis=0, tiled=True)


def total(blocks):
    return sum(b.astype(F32) for b in blocks)


def swap(block, axis):
    return lax.ppermute(block, axis, [(0, 1), (1, 0)])


def local(query_rows, key_rows, value_rows, out_weight, grad_out):
    core, half = lax.axis_index("core"), lax.axis_index("y_hi")
    where = jnp.stack([core, half]).astype(jnp.int32)
    square = ((256, 256), BF16)
    wide = ((256, 384), BF16)

    context, probs = call(
        attend, [square, ((2, 256, 256), F32)], [], 2**26, 2**20, 3, vmem_mib=60
    )(query_rows, key_rows, value_rows)
    ctx = lax.all_gather(context, "z", axis=0)

    weight = change_plane(out_weight.T)
    grad_out, context = lax.optimization_barrier((grad_out, context))
    far_cot = swap(grad_out, "y_hi")
    weight = lax.all_gather(weight, "y_lo", axis=0)
    weight, far_cot = lax.optimization_barrier((weight, far_cot))
    near = gather(weight, "x", 4)

    strips = ((2 * STRIP, 256), BF16)
    cot_mine, cot_theirs = call(
        turn_cot, [strips, strips], [pltpu.VMEM((384, 256), BF16)], 2**20, 2**20, 2, True, vmem_mib=4
    )(where, grad_out, far_cot)
    other_cot = swap(cot_theirs, "core")
    other_ctx = swap(ctx, "core")
    term = call(
        weight_term, [((4, 4, STRIP, 256), BF16)], [], 2**29, 2**22, 4, True, vmem_mib=10
    )(where, ctx, other_ctx, cot_mine, other_cot)[0]
    near, term = lax.optimization_barrier((near, term))
    far = swap(near, "core")
    term = scatter(term, "x")
    term = call(add_up, [((4, STRIP, 256), BF16)], [], 2**20, 2**21, 1, vmem_mib=4)(term)[0]

    dctx = call(
        project_back, [((8, 256, 256), BF16)], [], 2**29, 2**22, 4, True, vmem_mib=10
    )(where, cot_mine, cot_theirs, near, far)[0]
    dctx = lax.psum_scatter(dctx, "z", scatter_dimension=0, tiled=True)[0]
    keep, send = call(
        project,
        [wide, wide],
        [],
        2**29,
        2**22,
        3,
        True,
        vmem_mib=12,
    )(where, ctx, near, far)
    received = swap(send, "y_hi")
    layer_out = total([keep, received]).astype(BF16)
    term, received = lax.optimization_barrier((term, received))
    term = total(scatter(term, "y_lo")).astype(BF16)
    grad_weight = change_plane(term).T.astype(F32)
    grad_query, grad_key, grad_value = call(
        attend_back, [square] * 3, [], 2**27, 2**21, 5, vmem_mib=6
    )(query_rows, key_rows, value_rows, probs, dctx)
    return (layer_out, grad_query, grad_key, grad_value, grad_weight)


def solution(mesh):
    fine = Mesh(mesh.devices.reshape(SIZES), AXES)
    rows_cols, cols_rows = P(ROWS, COLS), P(COLS, ROWS)
    in_specs = (rows_cols, rows_cols, rows_cols, cols_rows, rows_cols)
    out_specs = (rows_cols, rows_cols, rows_cols, rows_cols, cols_rows)
    return jax.shard_map(local, mesh=fine, in_specs=in_specs, out_specs=out_specs, check_vma=False)
```

```python
import math

import jax
import jax.numpy as jnp
from jax import lax
from jax.experimental import pallas as pl
from jax.experimental.pallas import tpu as pltpu
from jax.sharding import Mesh, PartitionSpec as P

HEAD = 128
PATCHES = 256
FACTOR = 1.0 / math.sqrt(HEAD)
AXES = ("y_lo", "x", "core", "z", "y_hi")
SIZES = (4, 4, 2, 8, 2)
ROWS = ("y_lo", "x", "core")
COLS = ("z", "y_hi")
BF16 = jnp.bfloat16
F32 = jnp.float32
STRIP = 192
TN = (((0,), (0,)), ((), ()))
NT = (((1,), (1,)), ((), ()))
NN = (((1,), (0,)), ((), ()))


def dot(a, b, dims):
    return lax.dot_general(a, b, dims, preferred_element_type=F32)


def call(body, outs, scratch, flops, size, n_in, scalars=False, vmem_mib=40):
    vmem = pl.BlockSpec(memory_space=pltpu.VMEM)
    smem = pl.BlockSpec(memory_space=pltpu.SMEM)
    return pl.pallas_call(
        body,
        out_shape=[jax.ShapeDtypeStruct(s, t) for s, t in outs],
        in_specs=([smem] if scalars else []) + [vmem] * n_in,
        out_specs=[vmem] * len(outs),
        scratch_shapes=scratch,
        compiler_params=pltpu.CompilerParams(vmem_limit_bytes=vmem_mib * 2**20),
        cost_estimate=pl.CostEstimate(flops=flops, bytes_accessed=size, transcendentals=0),
    )


def attend(q_ref, k_ref, v_ref, ctx_ref, probs_ref):
    for h in range(2):
        cols = slice(h * HEAD, (h + 1) * HEAD)
        scores = dot(q_ref[:, cols], k_ref[:, cols], NT) * FACTOR
        exponent = jnp.exp(scores - jnp.max(scores, axis=-1, keepdims=True))
        probs = exponent / jnp.sum(exponent, axis=-1, keepdims=True)
        probs_ref[h] = probs
        ctx_ref[:, cols] = dot(probs.astype(BF16), v_ref[:, cols], NN).astype(BF16)


def attend_back(q_ref, k_ref, v_ref, probs_ref, dctx_ref, gq_ref, gk_ref, gv_ref):
    for h in range(2):
        cols = slice(h * HEAD, (h + 1) * HEAD)
        dctx = dctx_ref[:, cols]
        probs = probs_ref[h]
        gv_ref[:, cols] = dot(probs.astype(BF16), dctx, TN).astype(BF16)
        dprobs = dot(dctx, v_ref[:, cols], NT)
        center = jnp.sum(probs * dprobs, axis=-1, keepdims=True)
        dscores = (probs * (dprobs - center)).astype(BF16)
        gq_ref[:, cols] = (dot(dscores, k_ref[:, cols], NN) * FACTOR).astype(BF16)
        gk_ref[:, cols] = (dot(dscores, q_ref[:, cols], TN) * FACTOR).astype(BF16)


def turn_cot(where_ref, own_ref, far_ref, mine_ref, theirs_ref, work):
    core = where_ref[0]
    for slot, cot in enumerate((own_ref, far_ref)):
        work[...] = cot[...].astype(F32).T.astype(BF16)
        rows = slice(slot * STRIP, (slot + 1) * STRIP)
        mine_ref[rows, :] = work[pl.ds(pl.multiple_of(core * STRIP, 16), STRIP), :]
        theirs_ref[rows, :] = work[pl.ds(pl.multiple_of((1 - core) * STRIP, 16), STRIP), :]


def weight_term(where_ref, ctx_ref, other_ctx_ref, cot_ref, other_cot_ref, term_ref):
    half = where_ref[1]
    for z in range(8):
        term = dot(cot_ref[...], ctx_ref[z], NN) + dot(other_cot_ref[...], other_ctx_ref[z], NN)
        for slot in range(2):
            x = 2 * (z % 2) + (half if slot == 0 else 1 - half)
            term_ref[x, z // 2] = term[slot * STRIP : (slot + 1) * STRIP].astype(BF16)


def add_up(blocks_ref, sum_ref):
    for y in range(4):
        sum_ref[y] = sum(blocks_ref[x, y].astype(F32) for x in range(4)).astype(BF16)


def project_back(where_ref, mine_ref, theirs_ref, near_w_ref, far_w_ref, dctx_ref):
    half = where_ref[1]
    for z in range(8):
        part = None
        for slot in range(2):
            x = 2 * (z % 2) + (half if slot == 0 else 1 - half)
            rows = slice(slot * STRIP, (slot + 1) * STRIP)
            both = dot(mine_ref[rows, :], near_w_ref[x, z // 2], TN) + dot(
                theirs_ref[rows, :], far_w_ref[x, z // 2], TN
            )
            part = both if part is None else part + both
        dctx_ref[z] = part.astype(BF16)


def project(where_ref, ctx_ref, near_w_ref, far_w_ref, keep_ref, send_ref):
    core, half = where_ref[0], where_ref[1]
    for slot, out_ref in enumerate((keep_ref, send_ref)):
        x_lo = half if slot == 0 else 1 - half
        mine, theirs = (
            sum(dot(ctx_ref[z], w_ref[2 * (z % 2) + x_lo, z // 2], NT) for z in range(8)).astype(BF16)
            for w_ref in (near_w_ref, far_w_ref)
        )
        out_ref[:, :STRIP] = jnp.where(core == 0, mine, theirs)
        out_ref[:, STRIP:] = jnp.where(core == 0, theirs, mine)


def plane_pairs():
    pairs = []
    for y in range(4):
        for x in range(4):
            for z in range(8):
                there = (z // 2, 2 * (z % 2) + x % 2, 2 * y + x // 2)
                pairs.append(((y * 4 + x) * 8 + z, (there[0] * 4 + there[1]) * 8 + there[2]))
    return pairs


def change_plane(block):
    return lax.ppermute(block, ("y_lo", "x", "z"), plane_pairs())


def gather(block, axis, count):
    wide = jnp.broadcast_to(block[None], (count,) + block.shape)
    return lax.all_to_all(wide, axis, split_axis=0, concat_axis=0, tiled=True)


def scatter(blocks, axis):
    return lax.all_to_all(blocks, axis, split_axis=0, concat_axis=0, tiled=True)


def total(blocks):
    return sum(b.astype(F32) for b in blocks)


def swap(block, axis):
    return lax.ppermute(block, axis, [(0, 1), (1, 0)])


def local(query_rows, key_rows, value_rows, out_weight, grad_out):
    core, half = lax.axis_index("core"), lax.axis_index("y_hi")
    where = jnp.stack([core, half]).astype(jnp.int32)
    square = ((256, 256), BF16)
    wide = ((256, 384), BF16)

    context, probs = call(
        attend, [square, ((2, 256, 256), F32)], [], 2**26, 2**20, 3, vmem_mib=60
    )(query_rows, key_rows, value_rows)
    ctx = lax.all_gather(context, "z", axis=0)

    weight = change_plane(out_weight.T)
    grad_out, context = lax.optimization_barrier((grad_out, context))
    far_cot = swap(grad_out, "y_hi")
    weight = lax.all_gather(weight, "y_lo", axis=0)
    weight, far_cot = lax.optimization_barrier((weight, far_cot))
    near = gather(weight, "x", 4)

    strips = ((2 * STRIP, 256), BF16)
    cot_mine, cot_theirs = call(
        turn_cot, [strips, strips], [pltpu.VMEM((384, 256), BF16)], 2**20, 2**20, 2, True, vmem_mib=4
    )(where, grad_out, far_cot)
    other_cot = swap(cot_theirs, "core")
    other_ctx = swap(ctx, "core")
    term = call(
        weight_term, [((4, 4, STRIP, 256), BF16)], [], 2**29, 2**22, 4, True, vmem_mib=10
    )(where, ctx, other_ctx, cot_mine, other_cot)[0]
    near, term = lax.optimization_barrier((near, term))
    far = swap(near, "core")
    term = scatter(term, "x")
    term = call(add_up, [((4, STRIP, 256), BF16)], [], 2**20, 2**21, 1, vmem_mib=4)(term)[0]

    dctx = call(
        project_back, [((8, 256, 256), BF16)], [], 2**29, 2**22, 4, True, vmem_mib=10
    )(where, cot_mine, cot_theirs, near, far)[0]
    dctx = lax.psum_scatter(dctx, "z", scatter_dimension=0, tiled=True)[0]
    keep, send = call(
        project,
        [wide, wide],
        [],
        2**29,
        2**22,
        3,
        True,
        vmem_mib=12,
    )(where, ctx, near, far)
    received = swap(send, "y_hi")
    layer_out = total([keep, received]).astype(BF16)
    term, received = lax.optimization_barrier((term, received))
    term = total(scatter(term, "y_lo")).astype(BF16)
    term = change_plane(term)
    grad_query, grad_key, grad_value = call(
        attend_back, [square] * 3, [], 2**27, 2**21, 5, vmem_mib=6
    )(query_rows, key_rows, value_rows, probs, dctx)
    term, grad_query = lax.optimization_barrier((term, grad_query))
    grad_weight = term.T.astype(F32)
    return (layer_out, grad_query, grad_key, grad_value, grad_weight)


def solution(mesh):
    fine = Mesh(mesh.devices.reshape(SIZES), AXES)
    rows_cols, cols_rows = P(ROWS, COLS), P(COLS, ROWS)
    in_specs = (rows_cols, rows_cols, rows_cols, cols_rows, rows_cols)
    out_specs = (rows_cols, rows_cols, rows_cols, rows_cols, cols_rows)
    return jax.shard_map(local, mesh=fine, in_specs=in_specs, out_specs=out_specs, check_vma=False)
```

```python
import math

import jax
import jax.numpy as jnp
from jax import lax
from jax.experimental import pallas as pl
from jax.experimental.pallas import tpu as pltpu
from jax.sharding import Mesh, PartitionSpec as P

HEAD = 128
PATCHES = 256
FACTOR = 1.0 / math.sqrt(HEAD)
AXES = ("y_lo", "x", "core", "z", "y_hi")
SIZES = (4, 4, 2, 8, 2)
ROWS = ("y_lo", "x", "core")
COLS = ("z", "y_hi")
BF16 = jnp.bfloat16
F32 = jnp.float32
STRIP = 192
TN = (((0,), (0,)), ((), ()))
NT = (((1,), (1,)), ((), ()))
NN = (((1,), (0,)), ((), ()))


def dot(a, b, dims):
    return lax.dot_general(a, b, dims, preferred_element_type=F32)


def call(body, outs, scratch, flops, size, n_in, scalars=False, vmem_mib=40):
    vmem = pl.BlockSpec(memory_space=pltpu.VMEM)
    smem = pl.BlockSpec(memory_space=pltpu.SMEM)
    return pl.pallas_call(
        body,
        out_shape=[jax.ShapeDtypeStruct(s, t) for s, t in outs],
        in_specs=([smem] if scalars else []) + [vmem] * n_in,
        out_specs=[vmem] * len(outs),
        scratch_shapes=scratch,
        compiler_params=pltpu.CompilerParams(vmem_limit_bytes=vmem_mib * 2**20),
        cost_estimate=pl.CostEstimate(flops=flops, bytes_accessed=size, transcendentals=0),
    )


def attend(q_ref, k_ref, v_ref, ctx_ref, probs_ref):
    for h in range(2):
        cols = slice(h * HEAD, (h + 1) * HEAD)
        scores = dot(q_ref[:, cols], k_ref[:, cols], NT) * FACTOR
        exponent = jnp.exp(scores - jnp.max(scores, axis=-1, keepdims=True))
        probs = exponent / jnp.sum(exponent, axis=-1, keepdims=True)
        probs_ref[h] = probs
        ctx_ref[:, cols] = dot(probs.astype(BF16), v_ref[:, cols], NN).astype(BF16)


def attend_back(q_ref, k_ref, v_ref, probs_ref, dctx_ref, gq_ref, gk_ref, gv_ref):
    for h in range(2):
        cols = slice(h * HEAD, (h + 1) * HEAD)
        dctx = dctx_ref[:, cols]
        probs = probs_ref[h]
        gv_ref[:, cols] = dot(probs.astype(BF16), dctx, TN).astype(BF16)
        dprobs = dot(dctx, v_ref[:, cols], NT)
        center = jnp.sum(probs * dprobs, axis=-1, keepdims=True)
        dscores = (probs * (dprobs - center)).astype(BF16)
        gq_ref[:, cols] = (dot(dscores, k_ref[:, cols], NN) * FACTOR).astype(BF16)
        gk_ref[:, cols] = (dot(dscores, q_ref[:, cols], TN) * FACTOR).astype(BF16)


def turn_cot(where_ref, own_ref, far_ref, mine_ref, theirs_ref, work):
    core = where_ref[0]
    for slot, cot in enumerate((own_ref, far_ref)):
        work[...] = cot[...].astype(F32).T.astype(BF16)
        rows = slice(slot * STRIP, (slot + 1) * STRIP)
        mine_ref[rows, :] = work[pl.ds(pl.multiple_of(core * STRIP, 16), STRIP), :]
        theirs_ref[rows, :] = work[pl.ds(pl.multiple_of((1 - core) * STRIP, 16), STRIP), :]


def weight_term(where_ref, ctx_ref, other_ctx_ref, cot_ref, other_cot_ref, term_ref):
    half = where_ref[1]
    for z in range(8):
        term = dot(cot_ref[...], ctx_ref[z], NN) + dot(other_cot_ref[...], other_ctx_ref[z], NN)
        for slot in range(2):
            x = 2 * (z % 2) + (half if slot == 0 else 1 - half)
            term_ref[x, z // 2] = term[slot * STRIP : (slot + 1) * STRIP].astype(BF16)


def add_up(blocks_ref, sum_ref):
    for y in range(4):
        sum_ref[y] = sum(blocks_ref[x, y].astype(F32) for x in range(4)).astype(BF16)


def project_back(where_ref, mine_ref, theirs_ref, near_w_ref, far_w_ref, dctx_ref):
    half = where_ref[1]
    for z in range(8):
        part = None
        for slot in range(2):
            x = 2 * (z % 2) + (half if slot == 0 else 1 - half)
            rows = slice(slot * STRIP, (slot + 1) * STRIP)
            both = dot(mine_ref[rows, :], near_w_ref[x, z // 2], TN) + dot(
                theirs_ref[rows, :], far_w_ref[x, z // 2], TN
            )
            part = both if part is None else part + both
        dctx_ref[z] = part.astype(BF16)


def project(where_ref, ctx_ref, near_w_ref, far_w_ref, keep_ref, send_ref):
    core, half = where_ref[0], where_ref[1]
    for slot, out_ref in enumerate((keep_ref, send_ref)):
        x_lo = half if slot == 0 else 1 - half
        mine, theirs = (
            sum(dot(ctx_ref[z], w_ref[2 * (z % 2) + x_lo, z // 2], NT) for z in range(8)).astype(BF16)
            for w_ref in (near_w_ref, far_w_ref)
        )
        out_ref[:, :STRIP] = jnp.where(core == 0, mine, theirs)
        out_ref[:, STRIP:] = jnp.where(core == 0, theirs, mine)


def plane_pairs():
    pairs = []
    for y in range(4):
        for x in range(4):
            for z in range(8):
                there = (z // 2, 2 * (z % 2) + x % 2, 2 * y + x // 2)
                pairs.append(((y * 4 + x) * 8 + z, (there[0] * 4 + there[1]) * 8 + there[2]))
    return pairs


def change_plane(block):
    return lax.ppermute(block, ("y_lo", "x", "z"), plane_pairs())


def gather(block, axis, count):
    wide = jnp.broadcast_to(block[None], (count,) + block.shape)
    return lax.all_to_all(wide, axis, split_axis=0, concat_axis=0, tiled=True)


def scatter(blocks, axis):
    return lax.all_to_all(blocks, axis, split_axis=0, concat_axis=0, tiled=True)


def total(blocks):
    return sum(b.astype(F32) for b in blocks)


def swap(block, axis):
    return lax.ppermute(block, axis, [(0, 1), (1, 0)])


def local(query_rows, key_rows, value_rows, out_weight, grad_out):
    core, half = lax.axis_index("core"), lax.axis_index("y_hi")
    where = jnp.stack([core, half]).astype(jnp.int32)
    square = ((256, 256), BF16)
    wide = ((256, 384), BF16)

    context, probs = call(
        attend, [square, ((2, 256, 256), F32)], [], 2**26, 2**20, 3, vmem_mib=60
    )(query_rows, key_rows, value_rows)
    ctx = lax.all_gather(context, "z", axis=0)

    weight = change_plane(out_weight.T)
    grad_out, context = lax.optimization_barrier((grad_out, context))
    far_cot = swap(grad_out, "y_hi")
    weight = lax.all_gather(weight, "y_lo", axis=0)
    weight, far_cot = lax.optimization_barrier((weight, far_cot))
    near = gather(weight, "x", 4)

    strips = ((2 * STRIP, 256), BF16)
    cot_mine, cot_theirs = call(
        turn_cot, [strips, strips], [pltpu.VMEM((384, 256), BF16)], 2**20, 2**20, 2, True, vmem_mib=4
    )(where, grad_out, far_cot)
    other_cot = swap(cot_theirs, "core")
    other_ctx = swap(ctx, "core")
    term = call(
        weight_term, [((4, 4, STRIP, 256), BF16)], [], 2**29, 2**22, 4, True, vmem_mib=10
    )(where, ctx, other_ctx, cot_mine, other_cot)[0]
    near, term = lax.optimization_barrier((near, term))
    far = swap(near, "core")
    term = scatter(term, "x")
    term = call(add_up, [((4, STRIP, 256), BF16)], [], 2**20, 2**21, 1, vmem_mib=4)(term)[0]

    dctx = call(
        project_back, [((8, 256, 256), BF16)], [], 2**29, 2**22, 4, True, vmem_mib=10
    )(where, cot_mine, cot_theirs, near, far)[0]
    dctx = lax.psum_scatter(dctx, "z", scatter_dimension=0, tiled=True)[0]
    keep, send = call(
        project,
        [wide, wide],
        [],
        2**29,
        2**22,
        3,
        True,
        vmem_mib=12,
    )(where, ctx, near, far)
    received = swap(send, "y_hi")
    layer_out = total([keep, received]).astype(BF16)
    term, received = lax.optimization_barrier((term, received))
    term = total(scatter(term, "y_lo")).astype(BF16).T
    term = change_plane(term)
    grad_query, grad_key, grad_value = call(
        attend_back, [square] * 3, [], 2**27, 2**21, 5, vmem_mib=6
    )(query_rows, key_rows, value_rows, probs, dctx)
    term, grad_query = lax.optimization_barrier((term, grad_query))
    grad_weight = term.astype(F32)
    return (layer_out, grad_query, grad_key, grad_value, grad_weight)


def solution(mesh):
    fine = Mesh(mesh.devices.reshape(SIZES), AXES)
    rows_cols, cols_rows = P(ROWS, COLS), P(COLS, ROWS)
    in_specs = (rows_cols, rows_cols, rows_cols, cols_rows, rows_cols)
    out_specs = (rows_cols, rows_cols, rows_cols, rows_cols, cols_rows)
    return jax.shard_map(local, mesh=fine, in_specs=in_specs, out_specs=out_specs, check_vma=False)
```
